32 devices in a mesh: ctx: 8 (over z, y), fsdp: 4 (over x, core).
Axes of the slice: x: 2, y: 2, z: 4, core: 2. Of those that a mesh axis runs over, the one named last changes fastest.
Arguments:
- gate_in: bfloat16 [4096, 4096], P('ctx', 'fsdp'), may hold values from -6 to 6
- values: bfloat16 [4096, 4096], P('ctx', 'fsdp'), may hold values from -6 to 6
- gate_out: bfloat16 [4096, 4096], P('ctx', 'fsdp'), may hold values from -6 to 6
- bias: float32 [4096], P('fsdp'), may hold values from -4 to 4
- spectrum: bfloat16 [2, 8192, 4096], P(None, ('ctx', 'fsdp')), may hold values from -6 to 6
Outputs:
- gated: bfloat16 [4096, 4096], P('ctx', 'fsdp')
The draws below stay inside these ranges and needn't reach their ends.
All inputs are finite; a program needn't handle non-finite values.
Results may differ from the reference program's by a relative error of at most 0.0049.
Values may be sent and summed in bfloat16 or wider, within the bound.
A program may use at most 128 MiB of HBM per device.

```python
import jax
import jax.numpy as jnp
from jax import lax

D = 4096
TOK_DEV = 512
SEQ = 4096
FREQ = 8192
RADIX = 16
N_CTX = 8
N_FSDP = 4


def block_levels(stream_key, dims, cuts, least, largest):
    loudness = 1.0
    for dim, blocks in cuts:
        steps = jax.random.uniform(jax.random.fold_in(jax.random.fold_in(stream_key, 6), dim), (blocks,), jnp.float32, least / len(cuts), largest / len(cuts))
        loudness = loudness * jnp.repeat(jnp.exp(steps), dims[dim] // blocks).reshape((-1,) + (1,) * (len(dims) - 1 - dim))
    return loudness


def noise(key, shape, spread, reach, cuts=(), held_as=jnp.bfloat16):
    result = jax.random.normal(key, shape, jnp.float32) * spread
    if len(cuts) > 0:
        result = block_levels(key, shape, cuts, -0.22, 0.18) * result
    return jnp.clip(result, min=-reach, max=reach).astype(held_as)


def setup_inputs(seed: int = 0) -> dict:
    seeds = jax.random.split(jax.random.key(seed), 6)
    gate_in = noise(seeds[0], (SEQ, D), 1.0, 6.0, ((0, 8), (1, 4)))
    values = noise(seeds[1], (SEQ, D), 1.0, 6.0, ((0, 8), (1, 4)))
    gate_out = noise(seeds[2], (SEQ, D), 1.0, 6.0, ((0, 8), (1, 4)))
    bias = noise(seeds[3], (D,), 1.0, 4.0, ((0, 4),), jnp.float32)
    spectrum = noise(seeds[4], (2, FREQ, D), 1.0, 6.0, ((1, 32),))
    return {"gate_in": gate_in, "values": values, "gate_out": gate_out, "bias": bias, "spectrum": spectrum}


def reference(gate_in, values, gate_out, bias, spectrum):
    length = TOK_DEV * N_CTX
    frequency = jnp.arange(FREQ, dtype=jnp.int32)
    residue = (frequency % RADIX).astype(jnp.int32)
    half_radix = RADIX // 2
    slot_number = (residue >= half_radix).astype(jnp.int32)
    owner = jnp.where(residue < half_radix, residue, jnp.where(residue == half_radix, 0, RADIX - residue)).astype(jnp.int32)
    storage_row = (owner * (2 * TOK_DEV) + slot_number * TOK_DEV + frequency // RADIX).astype(jnp.int32)
    width_block = D // N_FSDP
    outputs = []
    for block_number in range(N_FSDP):
        low_col = block_number * width_block
        high_col = low_col + width_block
        product_in = (gate_in[:, low_col:high_col].astype(jnp.float32) * values[:, low_col:high_col].astype(jnp.float32)).astype(jnp.bfloat16)
        product_in = lax.optimization_barrier(product_in)
        signal = product_in.astype(jnp.float32)
        padded = jnp.concatenate([signal, jnp.zeros_like(signal)], axis=0)
        transformed = jnp.fft.fft(padded, axis=0)
        filter_real = jnp.take(spectrum[0, :, low_col:high_col], storage_row, axis=0).astype(jnp.float32)
        filter_imag = jnp.take(spectrum[1, :, low_col:high_col], storage_row, axis=0).astype(jnp.float32)
        response = lax.complex(filter_real, filter_imag)
        convolved = jnp.real(jnp.fft.ifft(transformed * response, axis=0))[:length]
        convolved = convolved + bias[low_col:high_col][None, :] * signal
        outputs.append((gate_out[:, low_col:high_col].astype(jnp.float32) * convolved).astype(jnp.bfloat16))
    return jnp.concatenate(outputs, axis=1)
```

```python
import functools
import math

import jax
import jax.numpy as jnp
import numpy as np
from jax import lax
from jax.experimental import pallas as pl
from jax.experimental.pallas import tpu as pltpu
from jax.sharding import Mesh, PartitionSpec as P


@functools.lru_cache(maxsize=None)
def transform_matrices(rows):
    j = np.arange(rows)
    angle = 2 * np.pi * (np.outer(j, j) % rows) / rows
    cos, sin = np.cos(angle), np.sin(angle)
    general = np.block([[cos, sin], [-sin, cos]])
    half = rows // 2
    m = np.arange(half)
    low = 2 * np.pi * (np.outer(m, j) % rows) / rows
    mid = 2 * np.pi * (np.outer(2 * m + 1, j) % (2 * rows)) / (2 * rows)
    zero = np.zeros((half, rows))
    low_sin = -np.sin(low)
    low_sin[0] = np.where(j % 2 == 0, 1.0, -1.0)
    first = np.block(
        [[np.cos(low), zero], [zero, np.cos(mid)], [low_sin, zero], [zero, -np.sin(mid)]]
    )
    both = np.stack([first, general])
    return both.astype(jnp.bfloat16), both.transpose(0, 2, 1).astype(jnp.bfloat16)


@functools.lru_cache(maxsize=None)
def mixing_weights(devices):
    c = np.arange(devices)
    angle = 2 * np.pi * (np.outer(c, c) % (2 * devices)) / (2 * devices)
    real, imag = np.cos(angle), -np.sin(angle)
    imag[0] = np.where(c % 2 == 0, 1.0, -1.0)
    return np.stack([real, imag]).astype(np.float32)


@functools.lru_cache(maxsize=None)
def twists(devices, rows):
    angle = 2 * np.pi * np.outer(np.arange(devices), np.arange(rows)) / (2 * devices * rows)
    return np.stack([np.cos(angle), np.sin(angle)], axis=1).astype(np.float32)


def convolve_kernel(scale, flag, weights, x, forward, inverse, twist, filt, out, total):
    c = pl.program_id(0)
    devices, rows, width = x.shape
    half = rows // 2

    mixed_real = jnp.zeros((rows, width), jnp.float32)
    mixed_imag = jnp.zeros((rows, width), jnp.float32)
    for n in range(devices):
        block = x[n].astype(jnp.float32)
        mixed_real += weights[0, c, n] * block
        mixed_imag += weights[1, c, n] * block
    tc = twist[0, 0]
    ts = twist[0, 1]
    turned = jnp.concatenate(
        [mixed_real * tc + mixed_imag * ts, mixed_imag * tc - mixed_real * ts]
    ).astype(jnp.bfloat16)
    freq = jnp.dot(forward[0], turned, preferred_element_type=jnp.float32)
    swap = flag[0]
    filt_real = jnp.concatenate([filt[0, swap, 0], filt[0, 1 - swap, 0]]).astype(jnp.float32)
    filt_imag = jnp.concatenate([filt[0, swap, 1], filt[0, 1 - swap, 1]]).astype(jnp.float32)
    fr, fi = freq[:rows], freq[rows:]
    single = jnp.logical_and(
        c == 0, lax.broadcasted_iota(jnp.int32, (rows, width), 0) == 0
    )
    cross = fi * filt_imag
    prod_real = fr * filt_real - jnp.where(single, 0.0, cross)
    prod_imag = jnp.where(single, cross, fr * filt_imag + fi * filt_real)
    prod = jnp.concatenate([prod_real, prod_imag]).astype(jnp.bfloat16)
    back = jnp.dot(inverse[0], prod, preferred_element_type=jnp.float32)
    br, bi = back[:rows], back[rows:]
    back_real = (br * tc - bi * ts) * scale
    back_imag = (br * ts + bi * tc) * scale

    @pl.when(c == 0)
    def _():
        for n in range(devices):
            total[n] = weights[0, c, n] * back_real + weights[1, c, n] * back_imag

    @pl.when(c > 0)
    def _():
        for n in range(devices):
            total[n] += weights[0, c, n] * back_real + weights[1, c, n] * back_imag

    @pl.when(c == devices - 1)
    def _():
        out[...] = total[...].astype(out.dtype)


def convolve(x, filt, flag):
    devices, rows, width = x.shape
    forward, inverse = transform_matrices(rows)
    weights = mixing_weights(devices)
    twist = np.broadcast_to(twists(devices, rows)[..., None], (devices, 2, rows, 1))
    twist = jnp.broadcast_to(jnp.asarray(twist), (devices, 2, rows, width))
    whole = lambda c: (0, 0, 0)
    matrix = pl.BlockSpec((1, 2 * rows, 2 * rows), lambda c: (jnp.minimum(c, 1), 0, 0))
    return pl.pallas_call(
        functools.partial(convolve_kernel, 1.0 / (2 * devices * rows)),
        grid=(devices,),
        in_specs=[
            pl.BlockSpec(memory_space=pltpu.SMEM),
            pl.BlockSpec(memory_space=pltpu.SMEM),
            pl.BlockSpec((devices, rows, width), whole),
            matrix,
            matrix,
            pl.BlockSpec((1, 2, rows, width), lambda c: (c, 0, 0, 0)),
            pl.BlockSpec((1, 2, 2, rows // 2, width), lambda c: (c, 0, 0, 0, 0)),
        ],
        out_specs=pl.BlockSpec((devices, rows, width), whole),
        out_shape=jax.ShapeDtypeStruct((devices, rows, width), jnp.bfloat16),
        scratch_shapes=[pltpu.VMEM((devices, rows, width), jnp.float32)],
        compiler_params=pltpu.CompilerParams(vmem_limit_bytes=56 * 2**20),
        cost_estimate=pl.CostEstimate(
            flops=16 * devices * rows * rows * width,
            bytes_accessed=16 * 2**20,
            transcendentals=0,
        ),
    )(flag, jnp.asarray(weights), x, jnp.asarray(forward), jnp.asarray(inverse), twist, filt)


def fold_filters(spectrum):
    hi, lo, position = lax.axis_index("hi"), lax.axis_index("lo"), lax.axis_index("ctx")
    devices = lax.axis_size("ctx")
    block = spectrum.shape[1]
    width = spectrum.shape[2] // 2
    first, second = spectrum[:, :, :width], spectrum[:, :, width:]
    upper = hi == 1
    kept = jnp.where(upper, second, first)
    sent = jnp.where(upper, first, second)
    got = lax.ppermute(sent, ("hi", "lo"), [(f, 3 - f) for f in range(4)])
    slot_a = jnp.where(upper, got, kept)
    slot_b = jnp.where(upper, kept, got)
    half = jnp.bitwise_xor(hi, lo)
    passed = jnp.where(half == 0, slot_b, slot_a)
    swapped = lax.ppermute(
        passed, ("ctx", "hi", "lo"), [(0, 1), (1, 0), (2, 3), (3, 2)]
    )
    edge = position == 0
    base = jnp.where(jnp.logical_and(edge, half == 1), slot_b, slot_a)
    mirrored = jnp.where(edge, swapped, slot_b)
    wrap = jnp.logical_and(edge, half == 0)
    row = lax.broadcasted_iota(jnp.int32, (block, block), 0)
    col = lax.broadcasted_iota(jnp.int32, (block, block), 1)
    flip = (row + col == jnp.where(wrap, block, block - 1)).astype(jnp.bfloat16)
    turned = jnp.einsum("ij,rjk->rik", flip, mirrored, preferred_element_type=jnp.float32)
    real = base[0].astype(jnp.float32) + turned[0]
    imag = base[1].astype(jnp.float32) - turned[1]
    at_edge = jnp.logical_and(wrap, lax.broadcasted_iota(jnp.int32, (block, 1), 0) == 0)
    imag = jnp.where(at_edge, mirrored[0, :1].astype(jnp.float32), imag)
    return jnp.stack([real, imag]).astype(jnp.bfloat16)


def body(gate_in, values, gate_out, bias, spectrum):
    devices = lax.axis_size("ctx")
    rows, channels = gate_in.shape
    width = channels // devices
    mixed = (gate_in.astype(jnp.float32) * values.astype(jnp.float32)).astype(jnp.bfloat16)
    mixed = lax.optimization_barrier(mixed)
    parts = mixed.reshape(rows, devices, width).transpose(1, 0, 2)
    sequence = lax.all_to_all(parts, "ctx", split_axis=0, concat_axis=0, tiled=True)

    folded = fold_filters(spectrum)
    block = folded.shape[1]
    pieces = folded.reshape(2, block, 2, devices, width).transpose(3, 2, 0, 1, 4)
    pieces = pieces.reshape(devices * 2, 2, block, width)
    filt = lax.all_to_all(pieces, ("ctx", "lo"), split_axis=0, concat_axis=0, tiled=True)
    filt = filt.reshape(devices, 2, 2, block, width)
    flag = lax.axis_index("hi").astype(jnp.int32).reshape(1)

    convolved = convolve(sequence, filt, flag)
    back = lax.all_to_all(convolved, "ctx", split_axis=0, concat_axis=0, tiled=True)
    back = back.transpose(1, 0, 2).reshape(rows, channels).astype(jnp.float32)
    total = back + bias[None, :] * mixed.astype(jnp.float32)
    return (gate_out.astype(jnp.float32) * total).astype(jnp.bfloat16)


def solution(mesh):
    ctx, fsdp = mesh.devices.shape
    split = Mesh(mesh.devices.reshape(ctx, fsdp // 2, 2), ("ctx", "hi", "lo"))
    tokens = P("ctx", ("hi", "lo"))
    return jax.shard_map(
        body,
        mesh=split,
        in_specs=(
            tokens,
            tokens,
            tokens,
            P(("hi", "lo")),
            P(None, ("ctx", "hi", "lo"), None),
        ),
        out_specs=tokens,
        check_vma=False,
    )
```

```python
import functools
import math

import jax
import jax.numpy as jnp
import numpy as np
from jax import lax
from jax.experimental import pallas as pl
from jax.experimental.pallas import tpu as pltpu
from jax.sharding import Mesh, PartitionSpec as P


@functools.lru_cache(maxsize=None)
def transform_matrices(rows):
    j = np.arange(rows)
    angle = 2 * np.pi * (np.outer(j, j) % rows) / rows
    cos, sin = np.cos(angle), np.sin(angle)
    general = np.block([[cos, sin], [-sin, cos]])
    half = rows // 2
    m = np.arange(half)
    low = 2 * np.pi * (np.outer(m, j) % rows) / rows
    mid = 2 * np.pi * (np.outer(2 * m + 1, j) % (2 * rows)) / (2 * rows)
    zero = np.zeros((half, rows))
    low_sin = -np.sin(low)
    low_sin[0] = np.where(j % 2 == 0, 1.0, -1.0)
    first = np.block(
        [[np.cos(low), zero], [zero, np.cos(mid)], [low_sin, zero], [zero, -np.sin(mid)]]
    )
    both = np.stack([first, general])
    return both.astype(jnp.bfloat16), both.transpose(0, 2, 1).astype(jnp.bfloat16)


@functools.lru_cache(maxsize=None)
def mixing_weights(devices):
    c = np.arange(devices)
    angle = 2 * np.pi * (np.outer(c, c) % (2 * devices)) / (2 * devices)
    real, imag = np.cos(angle), -np.sin(angle)
    imag[0] = np.where(c % 2 == 0, 1.0, -1.0)
    return np.stack([real, imag]).astype(np.float32)


@functools.lru_cache(maxsize=None)
def twists(devices, rows):
    angle = 2 * np.pi * np.outer(np.arange(devices), np.arange(rows)) / (2 * devices * rows)
    return np.stack([np.cos(angle), np.sin(angle)], axis=1).astype(np.float32)


def convolve_kernel(scale, flag, weights, x, forward, inverse, twist, filt, out, total):
    c = pl.program_id(0)
    devices, rows, width = x.shape
    half = rows // 2

    mixed_real = jnp.zeros((rows, width), jnp.float32)
    mixed_imag = jnp.zeros((rows, width), jnp.float32)
    for n in range(devices):
        block = x[n].astype(jnp.float32)
        mixed_real += weights[0, c, n] * block
        mixed_imag += weights[1, c, n] * block
    tc = twist[0, 0]
    ts = twist[0, 1]
    turned = jnp.concatenate(
        [mixed_real * tc + mixed_imag * ts, mixed_imag * tc - mixed_real * ts]
    ).astype(jnp.bfloat16)
    freq = jnp.dot(forward[0], turned, preferred_element_type=jnp.float32)
    swap = flag[0]
    filt_real = jnp.concatenate([filt[0, swap, 0], filt[0, 1 - swap, 0]]).astype(jnp.float32)
    filt_imag = jnp.concatenate([filt[0, swap, 1], filt[0, 1 - swap, 1]]).astype(jnp.float32)
    fr, fi = freq[:rows], freq[rows:]
    single = jnp.logical_and(
        c == 0, lax.broadcasted_iota(jnp.int32, (rows, width), 0) == 0
    )
    cross = fi * filt_imag
    prod_real = fr * filt_real - jnp.where(single, 0.0, cross)
    prod_imag = jnp.where(single, cross, fr * filt_imag + fi * filt_real)
    prod = jnp.concatenate([prod_real, prod_imag]).astype(jnp.bfloat16)
    back = jnp.dot(inverse[0], prod, preferred_element_type=jnp.float32)
    br, bi = back[:rows], back[rows:]
    back_real = (br * tc - bi * ts) * scale
    back_imag = (br * ts + bi * tc) * scale

    @pl.when(c == 0)
    def _():
        for n in range(devices):
            total[n] = weights[0, c, n] * back_real + weights[1, c, n] * back_imag

    @pl.when(c > 0)
    def _():
        for n in range(devices):
            total[n] += weights[0, c, n] * back_real + weights[1, c, n] * back_imag

    @pl.when(c == devices - 1)
    def _():
        out[...] = total[...].astype(out.dtype)


def convolve(x, filt, flag):
    devices, rows, width = x.shape
    forward, inverse = transform_matrices(rows)
    weights = mixing_weights(devices)
    twist = np.broadcast_to(twists(devices, rows)[..., None], (devices, 2, rows, width))
    twist = jnp.asarray(np.ascontiguousarray(twist))
    whole = lambda c: (0, 0, 0)
    matrix = pl.BlockSpec((1, 2 * rows, 2 * rows), lambda c: (jnp.minimum(c, 1), 0, 0))
    return pl.pallas_call(
        functools.partial(convolve_kernel, 1.0 / (2 * devices * rows)),
        grid=(devices,),
        in_specs=[
            pl.BlockSpec(memory_space=pltpu.SMEM),
            pl.BlockSpec(memory_space=pltpu.SMEM),
            pl.BlockSpec((devices, rows, width), whole),
            matrix,
            matrix,
            pl.BlockSpec((1, 2, rows, width), lambda c: (c, 0, 0, 0)),
            pl.BlockSpec((1, 2, 2, rows // 2, width), lambda c: (c, 0, 0, 0, 0)),
        ],
        out_specs=pl.BlockSpec((devices, rows, width), whole),
        out_shape=jax.ShapeDtypeStruct((devices, rows, width), jnp.bfloat16),
        scratch_shapes=[pltpu.VMEM((devices, rows, width), jnp.float32)],
        compiler_params=pltpu.CompilerParams(vmem_limit_bytes=56 * 2**20),
        cost_estimate=pl.CostEstimate(
            flops=16 * devices * rows * rows * width,
            bytes_accessed=16 * 2**20,
            transcendentals=0,
        ),
    )(flag, jnp.asarray(weights), x, jnp.asarray(forward), jnp.asarray(inverse), twist, filt)


def fold_filters(spectrum):
    hi, lo, position = lax.axis_index("hi"), lax.axis_index("lo"), lax.axis_index("ctx")
    devices = lax.axis_size("ctx")
    block = spectrum.shape[1]
    width = spectrum.shape[2] // 2
    first, second = spectrum[:, :, :width], spectrum[:, :, width:]
    upper = hi == 1
    kept = jnp.where(upper, second, first)
    sent = jnp.where(upper, first, second)
    got = lax.ppermute(sent, ("hi", "lo"), [(f, 3 - f) for f in range(4)])
    slot_a = jnp.where(upper, got, kept)
    slot_b = jnp.where(upper, kept, got)
    half = jnp.bitwise_xor(hi, lo)
    passed = jnp.where(half == 0, slot_b, slot_a)
    swapped = lax.ppermute(
        passed, ("ctx", "hi", "lo"), [(0, 1), (1, 0), (2, 3), (3, 2)]
    )
    edge = position == 0
    base = jnp.where(jnp.logical_and(edge, half == 1), slot_b, slot_a)
    mirrored = jnp.where(edge, swapped, slot_b)
    wrap = jnp.logical_and(edge, half == 0)
    row = lax.broadcasted_iota(jnp.int32, (block, block), 0)
    col = lax.broadcasted_iota(jnp.int32, (block, block), 1)
    flip = (row + col == jnp.where(wrap, block, block - 1)).astype(jnp.bfloat16)
    turned = jnp.einsum("ij,rjk->rik", flip, mirrored, preferred_element_type=jnp.float32)
    real = base[0].astype(jnp.float32) + turned[0]
    imag = base[1].astype(jnp.float32) - turned[1]
    at_edge = jnp.logical_and(wrap, lax.broadcasted_iota(jnp.int32, (block, 1), 0) == 0)
    imag = jnp.where(at_edge, mirrored[0, :1].astype(jnp.float32), imag)
    return jnp.stack([real, imag]).astype(jnp.bfloat16)


def exchange_kernel(gate_in, values, spectrum, sequence, filt, mixed, kept, got, swapped, pair,
                    folded, kept_sem, far_send, far_recv, swap_send, swap_recv, fold_send,
                    fold_recv, mix_send, mix_recv):
    me, hi, lo = lax.axis_index("ctx"), lax.axis_index("hi"), lax.axis_index("lo")
    devices, rows, width = sequence.shape
    block = spectrum.shape[1]
    group = devices * width
    edge = me == 0
    half = (hi + lo) % 2

    def columns(side, c, l):
        start = side * (2 * group) + l * group + c * width
        return spectrum.at[:, :, pl.ds(pl.multiple_of(start, 128), width)]

    def remote(src, dst, send, recv, target):
        return pltpu.make_async_remote_copy(
            src_ref=src, dst_ref=dst, send_sem=send, recv_sem=recv,
            device_id=target, device_id_type=pl.DeviceIdType.MESH,
        )

    def keep(c, l):
        return pltpu.make_async_copy(columns(hi, c, l), kept.at[c, l], kept_sem.at[c, l])

    def far(c, l):
        return remote(columns(1 - hi, c, l), got.at[c, l], far_send.at[c, l], far_recv.at[c, l],
                      (me, 1 - hi, 1 - lo))

    def swap(source, c, l):
        return remote(source.at[c, l], swapped.at[c, l], swap_send.at[c, l], swap_recv.at[c, l],
                      (me, hi, 1 - lo))

    def fold(c, l):
        return remote(folded.at[c, l], filt.at[me, lo], fold_send.at[c, l], fold_recv.at[me, lo],
                      (c, hi, l))

    def fold_here(c, l):
        return pltpu.make_async_copy(folded.at[c, l], filt.at[me, lo], fold_send.at[c, l])

    def mix(c):
        return remote(mixed.at[c], sequence.at[me], mix_send.at[c], mix_recv.at[me], (c, hi, lo))

    def mix_here():
        return pltpu.make_async_copy(mixed.at[me], sequence.at[me], mix_send.at[me])

    barrier = pltpu.get_barrier_semaphore()

    @pl.loop(0, devices)
    def _(c):
        for l in range(2):
            @pl.when(jnp.logical_or(c != me, lo != l))
            def _():
                pl.semaphore_signal(barrier, inc=1, device_id=(c, hi, l),
                                    device_id_type=pl.DeviceIdType.MESH)

    pl.semaphore_signal(barrier, inc=1, device_id=(me, 1 - hi, 1 - lo),
                        device_id_type=pl.DeviceIdType.MESH)

    @pl.loop(0, devices)
    def _(t):
        c = (me + 1 + t) % devices
        for l in range(2):
            keep(c, l).start()

    pl.semaphore_wait(barrier, 2 * devices)

    @pl.loop(0, devices)
    def _(t):
        c = (me + 1 + t) % devices
        for l in range(2):
            far(c, l).start()

    @pl.loop(0, devices)
    def _(t):
        c = (me + 1 + t) % devices
        place = pl.ds(pl.multiple_of(c * width, 128), width)
        mixed[c] = (
            gate_in[:, place].astype(jnp.float32) * values[:, place].astype(jnp.float32)
        ).astype(jnp.bfloat16)

        @pl.when(c != me)
        def _():
            mix(c).start()

        @pl.when(c == me)
        def _():
            mix_here().start()

    wrap = jnp.logical_and(edge, half == 0)
    row = lax.broadcasted_iota(jnp.int32, (block, block), 0)
    col = lax.broadcasted_iota(jnp.int32, (block, block), 1)
    flip = jnp.where(row + col == jnp.where(wrap, block, block - 1), 1.0, 0.0).astype(jnp.bfloat16)
    at_edge = jnp.logical_and(wrap, lax.broadcasted_iota(jnp.int32, (block, width), 0) == 0)
    base_got = jnp.where(edge, lo, hi) == 1

    @pl.loop(0, devices)
    def _(t):
        c = (me + 1 + t) % devices
        for l in range(2):
            keep(c, l).wait()

            @pl.when(jnp.logical_and(edge, lo == 1))
            def _():
                swap(kept, c, l).start()

        for l in range(2):
            far(c, l).wait_recv()

            @pl.when(jnp.logical_and(edge, lo == 0))
            def _():
                swap(got, c, l).start()

        for l in range(2):
            @pl.when(edge)
            def _():
                swap(kept, c, l).wait_recv()
                pair[...] = swapped[c, l]

            @pl.when(jnp.logical_and(me != 0, hi == 0))
            def _():
                pair[...] = got[c, l]

            @pl.when(jnp.logical_and(me != 0, hi == 1))
            def _():
                pair[...] = kept[c, l]

            base = jnp.where(base_got, got[c, l].astype(jnp.float32), kept[c, l].astype(jnp.float32))
            turned_real = jnp.dot(flip, pair[0], preferred_element_type=jnp.float32)
            turned_imag = jnp.dot(flip, pair[1], preferred_element_type=jnp.float32)
            real = base[0] + turned_real
            imag = jnp.where(at_edge, pair[0].astype(jnp.float32), base[1] - turned_imag)
            folded[c, l, 0] = real.astype(jnp.bfloat16)
            folded[c, l, 1] = imag.astype(jnp.bfloat16)
            here = jnp.logical_and(c == me, lo == l)

            @pl.when(here)
            def _():
                fold_here(c, l).start()

            @pl.when(jnp.logical_not(here))
            def _():
                fold(c, l).start()

    @pl.loop(0, devices)
    def _(c):
        @pl.when(c == me)
        def _():
            mix_here().wait()

        @pl.when(c != me)
        def _():
            mix(c).wait_send()
            remote(mixed.at[c], sequence.at[c], mix_send.at[c], mix_recv.at[c],
                   (c, hi, lo)).wait_recv()

        for l in range(2):
            far(c, l).wait_send()

            @pl.when(edge)
            def _():
                swap(kept, c, l).wait_send()

            here = jnp.logical_and(c == me, lo == l)

            @pl.when(here)
            def _():
                fold_here(c, l).wait()

            @pl.when(jnp.logical_not(here))
            def _():
                fold(c, l).wait_send()
                remote(folded.at[c, l], filt.at[c, l], fold_send.at[c, l], fold_recv.at[c, l],
                       (c, hi, l)).wait_recv()


def exchange(gate_in, values, spectrum):
    devices = lax.axis_size("ctx")
    rows, channels = gate_in.shape
    width = channels // devices
    block = spectrum.shape[1]
    tile = (devices, 2, 2, block, width)
    dma = pltpu.SemaphoreType.DMA
    here = pl.BlockSpec(memory_space=pltpu.VMEM)
    anywhere = pl.BlockSpec(memory_space=pl.ANY)
    return pl.pallas_call(
        exchange_kernel,
        in_specs=[here, here, anywhere],
        out_specs=[anywhere, anywhere],
        out_shape=[
            jax.ShapeDtypeStruct((devices, rows, width), jnp.bfloat16),
            jax.ShapeDtypeStruct(tile, jnp.bfloat16),
        ],
        scratch_shapes=[
            pltpu.VMEM((devices, rows, width), jnp.bfloat16),
            pltpu.VMEM(tile, jnp.bfloat16),
            pltpu.VMEM(tile, jnp.bfloat16),
            pltpu.VMEM(tile, jnp.bfloat16),
            pltpu.VMEM((2, block, width), jnp.bfloat16),
            pltpu.VMEM(tile, jnp.bfloat16),
            *[dma((devices, 2))] * 7,
            dma((devices,)),
            dma((devices,)),
        ],
        compiler_params=pltpu.CompilerParams(
            collective_id=0, has_side_effects=True, vmem_limit_bytes=48 * 2**20
        ),
        cost_estimate=pl.CostEstimate(flops=10**9, bytes_accessed=16 * 2**20, transcendentals=0),
    )(gate_in, values, spectrum)


def exchange_small(mixed, spectrum):
    devices = lax.axis_size("ctx")
    rows, channels = mixed.shape
    width = channels // devices
    parts = mixed.reshape(rows, devices, width).transpose(1, 0, 2)
    sequence = lax.all_to_all(parts, "ctx", split_axis=0, concat_axis=0, tiled=True)

    folded = fold_filters(spectrum)
    block = folded.shape[1]
    pieces = folded.reshape(2, block, 2, devices, width).transpose(3, 2, 0, 1, 4)
    pieces = pieces.reshape(devices * 2, 2, block, width)
    filt = lax.all_to_all(pieces, ("ctx", "lo"), split_axis=0, concat_axis=0, tiled=True)
    filt = filt.reshape(devices, 2, 2, block, width)
    return sequence, filt


def body(gate_in, values, gate_out, bias, spectrum):
    devices = lax.axis_size("ctx")
    rows, channels = gate_in.shape
    width = channels // devices
    mixed = (gate_in.astype(jnp.float32) * values.astype(jnp.float32)).astype(jnp.bfloat16)
    mixed = lax.optimization_barrier(mixed)
    if width % 128 == 0:
        sequence, filt = exchange(gate_in, values, spectrum)
    else:
        sequence, filt = exchange_small(mixed, spectrum)
    flag = lax.axis_index("hi").astype(jnp.int32).reshape(1)

    convolved = convolve(sequence, filt, flag)
    back = lax.all_to_all(convolved, "ctx", split_axis=0, concat_axis=0, tiled=True)
    back = back.transpose(1, 0, 2).reshape(rows, channels).astype(jnp.float32)
    total = back + bias[None, :] * mixed.astype(jnp.float32)
    return (gate_out.astype(jnp.float32) * total).astype(jnp.bfloat16)


def solution(mesh):
    ctx, fsdp = mesh.devices.shape
    split = Mesh(mesh.devices.reshape(ctx, fsdp // 2, 2), ("ctx", "hi", "lo"))
    tokens = P("ctx", ("hi", "lo"))
    return jax.shard_map(
        body,
        mesh=split,
        in_specs=(
            tokens,
            tokens,
            tokens,
            P(("hi", "lo")),
            P(None, ("ctx", "hi", "lo"), None),
        ),
        out_specs=tokens,
        check_vma=False,
    )
```

```python
import functools
import math

import jax
import jax.numpy as jnp
import numpy as np
from jax import lax
from jax.experimental import pallas as pl
from jax.experimental.pallas import tpu as pltpu
from jax.sharding import Mesh, PartitionSpec as P


@functools.lru_cache(maxsize=None)
def transform_matrices(rows):
    j = np.arange(rows)
    angle = 2 * np.pi * (np.outer(j, j) % rows) / rows
    cos, sin = np.cos(angle), np.sin(angle)
    general = np.block([[cos, sin], [-sin, cos]])
    half = rows // 2
    m = np.arange(half)
    low = 2 * np.pi * (np.outer(m, j) % rows) / rows
    mid = 2 * np.pi * (np.outer(2 * m + 1, j) % (2 * rows)) / (2 * rows)
    zero = np.zeros((half, rows))
    low_sin = -np.sin(low)
    low_sin[0] = np.where(j % 2 == 0, 1.0, -1.0)
    first = np.block(
        [[np.cos(low), zero], [zero, np.cos(mid)], [low_sin, zero], [zero, -np.sin(mid)]]
    )
    both = np.stack([first, general])
    return both.astype(jnp.bfloat16), both.transpose(0, 2, 1).astype(jnp.bfloat16)


@functools.lru_cache(maxsize=None)
def mixing_weights(devices):
    c = np.arange(devices)
    angle = 2 * np.pi * (np.outer(c, c) % (2 * devices)) / (2 * devices)
    real, imag = np.cos(angle), -np.sin(angle)
    imag[0] = np.where(c % 2 == 0, 1.0, -1.0)
    return np.stack([real, imag]).astype(np.float32)


@functools.lru_cache(maxsize=None)
def twists(devices, rows):
    angle = 2 * np.pi * np.outer(np.arange(devices), np.arange(rows)) / (2 * devices * rows)
    return np.stack([np.cos(angle), np.sin(angle)], axis=1).astype(np.float32)


def convolve_kernel(scale, flag, weights, x, forward, inverse, twist, filt, out, total):
    c = pl.program_id(0)
    devices, rows, width = x.shape
    half = rows // 2

    mixed_real = jnp.zeros((rows, width), jnp.float32)
    mixed_imag = jnp.zeros((rows, width), jnp.float32)
    for n in range(devices):
        block = x[n].astype(jnp.float32)
        mixed_real += weights[0, c, n] * block
        mixed_imag += weights[1, c, n] * block
    tc = twist[0, 0]
    ts = twist[0, 1]
    turned = jnp.concatenate(
        [mixed_real * tc + mixed_imag * ts, mixed_imag * tc - mixed_real * ts]
    ).astype(jnp.bfloat16)
    freq = jnp.dot(forward[0], turned, preferred_element_type=jnp.float32)
    swap = flag[0]
    filt_real = jnp.concatenate([filt[0, swap, 0], filt[0, 1 - swap, 0]]).astype(jnp.float32)
    filt_imag = jnp.concatenate([filt[0, swap, 1], filt[0, 1 - swap, 1]]).astype(jnp.float32)
    fr, fi = freq[:rows], freq[rows:]
    single = jnp.logical_and(
        c == 0, lax.broadcasted_iota(jnp.int32, (rows, width), 0) == 0
    )
    cross = fi * filt_imag
    prod_real = fr * filt_real - jnp.where(single, 0.0, cross)
    prod_imag = jnp.where(single, cross, fr * filt_imag + fi * filt_real)
    prod = jnp.concatenate([prod_real, prod_imag]).astype(jnp.bfloat16)
    back = jnp.dot(inverse[0], prod, preferred_element_type=jnp.float32)
    br, bi = back[:rows], back[rows:]
    back_real = (br * tc - bi * ts) * scale
    back_imag = (br * ts + bi * tc) * scale

    @pl.when(c == 0)
    def _():
        for n in range(devices):
            total[n] = weights[0, c, n] * back_real + weights[1, c, n] * back_imag

    @pl.when(c > 0)
    def _():
        for n in range(devices):
            total[n] += weights[0, c, n] * back_real + weights[1, c, n] * back_imag

    @pl.when(c == devices - 1)
    def _():
        out[...] = total[...].astype(out.dtype)


def convolve(x, filt, flag):
    devices, rows, width = x.shape
    forward, inverse = transform_matrices(rows)
    weights = mixing_weights(devices)
    twist = np.broadcast_to(twists(devices, rows)[..., None], (devices, 2, rows, width))
    twist = jnp.asarray(np.ascontiguousarray(twist))
    whole = lambda c: (0, 0, 0)
    matrix = pl.BlockSpec((1, 2 * rows, 2 * rows), lambda c: (jnp.minimum(c, 1), 0, 0))
    return pl.pallas_call(
        functools.partial(convolve_kernel, 1.0 / (2 * devices * rows)),
        grid=(devices,),
        in_specs=[
            pl.BlockSpec(memory_space=pltpu.SMEM),
            pl.BlockSpec(memory_space=pltpu.SMEM),
            pl.BlockSpec((devices, rows, width), whole),
            matrix,
            matrix,
            pl.BlockSpec((1, 2, rows, width), lambda c: (c, 0, 0, 0)),
            pl.BlockSpec((1, 2, 2, rows // 2, width), lambda c: (c, 0, 0, 0, 0)),
        ],
        out_specs=pl.BlockSpec((devices, rows, width), whole),
        out_shape=jax.ShapeDtypeStruct((devices, rows, width), jnp.bfloat16),
        scratch_shapes=[pltpu.VMEM((devices, rows, width), jnp.float32)],
        compiler_params=pltpu.CompilerParams(vmem_limit_bytes=56 * 2**20),
        cost_estimate=pl.CostEstimate(
            flops=16 * devices * rows * rows * width,
            bytes_accessed=16 * 2**20,
            transcendentals=0,
        ),
    )(flag, jnp.asarray(weights), x, jnp.asarray(forward), jnp.asarray(inverse), twist, filt)


def fold_filters(spectrum):
    hi, lo, position = lax.axis_index("hi"), lax.axis_index("lo"), lax.axis_index("ctx")
    devices = lax.axis_size("ctx")
    block = spectrum.shape[1]
    width = spectrum.shape[2] // 2
    first, second = spectrum[:, :, :width], spectrum[:, :, width:]
    upper = hi == 1
    kept = jnp.where(upper, second, first)
    sent = jnp.where(upper, first, second)
    got = lax.ppermute(sent, ("hi", "lo"), [(f, 3 - f) for f in range(4)])
    slot_a = jnp.where(upper, got, kept)
    slot_b = jnp.where(upper, kept, got)
    half = jnp.bitwise_xor(hi, lo)
    passed = jnp.where(half == 0, slot_b, slot_a)
    swapped = lax.ppermute(
        passed, ("ctx", "hi", "lo"), [(0, 1), (1, 0), (2, 3), (3, 2)]
    )
    edge = position == 0
    base = jnp.where(jnp.logical_and(edge, half == 1), slot_b, slot_a)
    mirrored = jnp.where(edge, swapped, slot_b)
    wrap = jnp.logical_and(edge, half == 0)
    row = lax.broadcasted_iota(jnp.int32, (block, block), 0)
    col = lax.broadcasted_iota(jnp.int32, (block, block), 1)
    flip = (row + col == jnp.where(wrap, block, block - 1)).astype(jnp.bfloat16)
    turned = jnp.einsum("ij,rjk->rik", flip, mirrored, preferred_element_type=jnp.float32)
    real = base[0].astype(jnp.float32) + turned[0]
    imag = base[1].astype(jnp.float32) - turned[1]
    at_edge = jnp.logical_and(wrap, lax.broadcasted_iota(jnp.int32, (block, 1), 0) == 0)
    imag = jnp.where(at_edge, mirrored[0, :1].astype(jnp.float32), imag)
    return jnp.stack([real, imag]).astype(jnp.bfloat16)


def fused_kernel(scale, weights, gate_in, values, gate_out, bias, spectrum, forward_in, inverse_in,
                 twist_in, out, sequence, filt, mixed, kept, got, swapped, pair, folded, forward,
                 inverse, twist, freq, total, leaving, arrived, kept_sem, far_send, far_recv,
                 swap_send, swap_recv, fold_send, fold_recv, mix_send, mix_recv, back_send,
                 back_recv, table_sem):
    me, hi, lo = lax.axis_index("ctx"), lax.axis_index("hi"), lax.axis_index("lo")
    devices, rows, width = sequence.shape
    block = spectrum.shape[1]
    group = devices * width
    edge = me == 0
    half = (hi + lo) % 2

    def columns(side, c, l):
        start = side * (2 * group) + l * group + c * width
        return spectrum.at[:, :, pl.ds(pl.multiple_of(start, 128), width)]

    def remote(src, dst, send, recv, target):
        return pltpu.make_async_remote_copy(
            src_ref=src, dst_ref=dst, send_sem=send, recv_sem=recv,
            device_id=target, device_id_type=pl.DeviceIdType.MESH,
        )

    def keep(c, l):
        return pltpu.make_async_copy(columns(hi, c, l), kept.at[c, l], kept_sem.at[c, l])

    def far(c, l):
        return remote(columns(1 - hi, c, l), got.at[c, l], far_send.at[c, l], far_recv.at[c, l],
                      (me, 1 - hi, 1 - lo))

    def swap(source, c, l):
        return remote(source.at[c, l], swapped.at[c, l], swap_send.at[c, l], swap_recv.at[c, l],
                      (me, hi, 1 - lo))

    def fold(c, l):
        return remote(folded.at[c, l], filt.at[me, lo], fold_send.at[c, l], fold_recv.at[me, lo],
                      (c, hi, l))

    def fold_here(c, l):
        return pltpu.make_async_copy(folded.at[c, l], filt.at[me, lo], fold_send.at[c, l])

    def mix(c):
        return remote(mixed.at[c], sequence.at[me], mix_send.at[c], mix_recv.at[me], (c, hi, lo))

    def mix_here():
        return pltpu.make_async_copy(mixed.at[me], sequence.at[me], mix_send.at[me])

    def give_back(n):
        return remote(leaving.at[n], arrived.at[me], back_send.at[n], back_recv.at[me],
                      (n, hi, lo))

    tables = [
        pltpu.make_async_copy(src, dst, table_sem.at[i])
        for i, (src, dst) in enumerate(
            ((forward_in, forward), (inverse_in, inverse), (twist_in, twist))
        )
    ]

    barrier = pltpu.get_barrier_semaphore()

    @pl.loop(0, devices)
    def _(c):
        for l in range(2):
            @pl.when(jnp.logical_or(c != me, lo != l))
            def _():
                pl.semaphore_signal(barrier, inc=1, device_id=(c, hi, l),
                                    device_id_type=pl.DeviceIdType.MESH)

    pl.semaphore_signal(barrier, inc=1, device_id=(me, 1 - hi, 1 - lo),
                        device_id_type=pl.DeviceIdType.MESH)

    @pl.loop(0, devices)
    def _(t):
        c = (me + 1 + t) % devices
        for l in range(2):
            keep(c, l).start()

    pl.semaphore_wait(barrier, 2 * devices)

    @pl.loop(0, devices)
    def _(t):
        c = (me + 1 + t) % devices
        for l in range(2):
            far(c, l).start()

    @pl.loop(0, devices)
    def _(t):
        c = (me + 1 + t) % devices
        place = pl.ds(pl.multiple_of(c * width, 128), width)
        mixed[c] = (
            gate_in[:, place].astype(jnp.float32) * values[:, place].astype(jnp.float32)
        ).astype(jnp.bfloat16)

        @pl.when(c != me)
        def _():
            mix(c).start()

        @pl.when(c == me)
        def _():
            mix_here().start()

    for table in tables:
        table.start()

    wrap = jnp.logical_and(edge, half == 0)
    row = lax.broadcasted_iota(jnp.int32, (block, block), 0)
    col = lax.broadcasted_iota(jnp.int32, (block, block), 1)
    flip = jnp.where(row + col == jnp.where(wrap, block, block - 1), 1.0, 0.0).astype(jnp.bfloat16)
    at_edge = jnp.logical_and(wrap, lax.broadcasted_iota(jnp.int32, (block, width), 0) == 0)
    base_got = jnp.where(edge, lo, hi) == 1

    def fold_step(t):
        c = (me + 1 + t) % devices
        for l in range(2):
            keep(c, l).wait()

            @pl.when(jnp.logical_and(edge, lo == 1))
            def _():
                swap(kept, c, l).start()

        for l in range(2):
            far(c, l).wait_recv()

            @pl.when(jnp.logical_and(edge, lo == 0))
            def _():
                swap(got, c, l).start()

        for l in range(2):
            @pl.when(edge)
            def _():
                swap(kept, c, l).wait_recv()
                pair[...] = swapped[c, l]

            @pl.when(jnp.logical_and(me != 0, hi == 0))
            def _():
                pair[...] = got[c, l]

            @pl.when(jnp.logical_and(me != 0, hi == 1))
            def _():
                pair[...] = kept[c, l]

            base = jnp.where(base_got, got[c, l].astype(jnp.float32), kept[c, l].astype(jnp.float32))
            turned_real = jnp.dot(flip, pair[0], preferred_element_type=jnp.float32)
            turned_imag = jnp.dot(flip, pair[1], preferred_element_type=jnp.float32)
            real = base[0] + turned_real
            imag = jnp.where(at_edge, pair[0].astype(jnp.float32), base[1] - turned_imag)
            folded[c, l, 0] = real.astype(jnp.bfloat16)
            folded[c, l, 1] = imag.astype(jnp.bfloat16)
            here = jnp.logical_and(c == me, lo == l)

            @pl.when(here)
            def _():
                fold_here(c, l).start()

            @pl.when(jnp.logical_not(here))
            def _():
                fold(c, l).start()

    def forward_step(c):
        real = jnp.zeros((rows, width), jnp.float32)
        imag = jnp.zeros((rows, width), jnp.float32)
        for n in range(devices):
            part = sequence[n].astype(jnp.float32)
            real += weights[0, c, n] * part
            imag += weights[1, c, n] * part
        tc, ts = twist[c, 0], twist[c, 1]
        turned = jnp.concatenate([real * tc + imag * ts, imag * tc - real * ts])
        freq[c] = jnp.dot(
            forward[jnp.minimum(c, 1)], turned.astype(jnp.bfloat16),
            preferred_element_type=jnp.float32,
        )

    def inverse_step(c):
        filt_real = jnp.concatenate([filt[c, hi, 0], filt[c, 1 - hi, 0]]).astype(jnp.float32)
        filt_imag = jnp.concatenate([filt[c, hi, 1], filt[c, 1 - hi, 1]]).astype(jnp.float32)
        fr, fi = freq[c, :rows], freq[c, rows:]
        top = lax.broadcasted_iota(jnp.int32, (rows, width), 0) == 0
        single = jnp.logical_and(c == 0, top)
        cross = fi * filt_imag
        prod_real = fr * filt_real - jnp.where(single, 0.0, cross)
        prod_imag = jnp.where(single, cross, fr * filt_imag + fi * filt_real)
        prod = jnp.concatenate([prod_real, prod_imag]).astype(jnp.bfloat16)
        back = jnp.dot(inverse[jnp.minimum(c, 1)], prod, preferred_element_type=jnp.float32)
        tc, ts = twist[c, 0] * scale, twist[c, 1] * scale
        br, bi = back[:rows], back[rows:]
        real = br * tc - bi * ts
        imag = br * ts + bi * tc
        for n in range(devices):
            total[n] += weights[0, c, n] * real + weights[1, c, n] * imag

    early = devices // 2

    @pl.loop(0, early)
    def _(t):
        fold_step(t)

    for table in tables:
        table.wait()

    @pl.loop(0, devices)
    def _(c):
        total[c] = jnp.zeros((rows, width), jnp.float32)

        @pl.when(c == me)
        def _():
            mix_here().wait()

        @pl.when(c != me)
        def _():
            remote(mixed.at[c], sequence.at[c], mix_send.at[c], mix_recv.at[c],
                   (c, hi, lo)).wait_recv()

    @pl.loop(early, devices)
    def _(t):
        fold_step(t)

        @pl.loop(0, 2)
        def _(i):
            forward_step(2 * (t - early) + i)

    @pl.loop(0, devices)
    def _(s):
        c = (me + (2 * devices - 1) - s) % devices
        for l in range(2):
            here = jnp.logical_and(c == me, lo == l)

            @pl.when(here)
            def _():
                fold_here(c, l).wait()

            @pl.when(jnp.logical_not(here))
            def _():
                remote(folded.at[c, l], filt.at[c, l], fold_send.at[c, l], fold_recv.at[c, l],
                       (c, hi, l)).wait_recv()

        inverse_step(c)

    @pl.loop(0, devices)
    def _(t):
        n = (me + 1 + t) % devices
        leaving[n] = total[n].astype(jnp.bfloat16)

        @pl.when(n != me)
        def _():
            give_back(n).start()

    @pl.loop(0, devices)
    def _(s):
        c = (me + (2 * devices) - s) % devices
        place = pl.ds(pl.multiple_of(c * width, 128), width)

        @pl.when(c == me)
        def _():
            arrived[c] = leaving[c]

        @pl.when(c != me)
        def _():
            remote(leaving.at[c], arrived.at[c], back_send.at[c], back_recv.at[c],
                   (c, hi, lo)).wait_recv()

        skip = bias[:, place] * mixed[c].astype(jnp.float32)
        out[:, place] = (
            gate_out[:, place].astype(jnp.float32) * (arrived[c].astype(jnp.float32) + skip)
        ).astype(out.dtype)

    @pl.loop(0, devices)
    def _(c):
        @pl.when(c != me)
        def _():
            mix(c).wait_send()
            give_back(c).wait_send()

        for l in range(2):
            far(c, l).wait_send()

            @pl.when(edge)
            def _():
                swap(kept, c, l).wait_send()

            @pl.when(jnp.logical_or(c != me, lo != l))
            def _():
                fold(c, l).wait_send()


def fused(gate_in, values, gate_out, bias, spectrum):
    devices = lax.axis_size("ctx")
    rows, channels = gate_in.shape
    width = channels // devices
    block = spectrum.shape[1]
    forward, inverse = transform_matrices(rows)
    twist = np.broadcast_to(twists(devices, rows)[..., None], (devices, 2, rows, width))
    tile = (devices, 2, 2, block, width)
    whole = (devices, rows, width)
    dma = pltpu.SemaphoreType.DMA
    here = pl.BlockSpec(memory_space=pltpu.VMEM)
    anywhere = pl.BlockSpec(memory_space=pl.ANY)
    return pl.pallas_call(
        functools.partial(fused_kernel, 1.0 / (2 * devices * rows)),
        in_specs=[pl.BlockSpec(memory_space=pltpu.SMEM)] + [here] * 4 + [anywhere] * 4,
        out_specs=here,
        out_shape=jax.ShapeDtypeStruct((rows, channels), jnp.bfloat16),
        scratch_shapes=[
            pltpu.VMEM(whole, jnp.bfloat16),
            pltpu.VMEM(tile, jnp.bfloat16),
            pltpu.VMEM(whole, jnp.bfloat16),
            pltpu.VMEM(tile, jnp.bfloat16),
            pltpu.VMEM(tile, jnp.bfloat16),
            pltpu.VMEM(tile, jnp.bfloat16),
            pltpu.VMEM((2, block, width), jnp.bfloat16),
            pltpu.VMEM(tile, jnp.bfloat16),
            pltpu.VMEM((2, 2 * rows, 2 * rows), jnp.bfloat16),
            pltpu.VMEM((2, 2 * rows, 2 * rows), jnp.bfloat16),
            pltpu.VMEM((devices, 2, rows, width), jnp.float32),
            pltpu.VMEM((devices, 2 * rows, width), jnp.float32),
            pltpu.VMEM(whole, jnp.float32),
            pltpu.VMEM(whole, jnp.bfloat16),
            pltpu.VMEM(whole, jnp.bfloat16),
            *[dma((devices, 2))] * 7,
            *[dma((devices,))] * 4,
            dma((3,)),
        ],
        compiler_params=pltpu.CompilerParams(
            collective_id=0, has_side_effects=True, vmem_limit_bytes=58 * 2**20
        ),
        cost_estimate=pl.CostEstimate(
            flops=16 * devices * rows * rows * width + 10**9,
            bytes_accessed=24 * 2**20,
            transcendentals=0,
        ),
    )(
        jnp.asarray(mixing_weights(devices)), gate_in, values, gate_out, bias.reshape(1, channels),
        spectrum, jnp.asarray(forward), jnp.asarray(inverse),
        jnp.asarray(np.ascontiguousarray(twist)),
    )


def exchange_small(mixed, spectrum):
    devices = lax.axis_size("ctx")
    rows, channels = mixed.shape
    width = channels // devices
    parts = mixed.reshape(rows, devices, width).transpose(1, 0, 2)
    sequence = lax.all_to_all(parts, "ctx", split_axis=0, concat_axis=0, tiled=True)

    folded = fold_filters(spectrum)
    block = folded.shape[1]
    pieces = folded.reshape(2, block, 2, devices, width).transpose(3, 2, 0, 1, 4)
    pieces = pieces.reshape(devices * 2, 2, block, width)
    filt = lax.all_to_all(pieces, ("ctx", "lo"), split_axis=0, concat_axis=0, tiled=True)
    filt = filt.reshape(devices, 2, 2, block, width)
    return sequence, filt


def body(gate_in, values, gate_out, bias, spectrum):
    devices = lax.axis_size("ctx")
    rows, channels = gate_in.shape
    width = channels // devices
    if width % 128 == 0:
        return fused(gate_in, values, gate_out, bias, spectrum)
    mixed = (gate_in.astype(jnp.float32) * values.astype(jnp.float32)).astype(jnp.bfloat16)
    mixed = lax.optimization_barrier(mixed)
    sequence, filt = exchange_small(mixed, spectrum)
    flag = lax.axis_index("hi").astype(jnp.int32).reshape(1)

    convolved = convolve(sequence, filt, flag)
    back = lax.all_to_all(convolved, "ctx", split_axis=0, concat_axis=0, tiled=True)
    back = back.transpose(1, 0, 2).reshape(rows, channels).astype(jnp.float32)
    total = back + bias[None, :] * mixed.astype(jnp.float32)
    return (gate_out.astype(jnp.float32) * total).astype(jnp.bfloat16)


def solution(mesh):
    ctx, fsdp = mesh.devices.shape
    split = Mesh(mesh.devices.reshape(ctx, fsdp // 2, 2), ("ctx", "hi", "lo"))
    tokens = P("ctx", ("hi", "lo"))
    return jax.shard_map(
        body,
        mesh=split,
        in_specs=(
            tokens,
            tokens,
            tokens,
            P(("hi", "lo")),
            P(None, ("ctx", "hi", "lo"), None),
        ),
        out_specs=tokens,
        check_vma=False,
    )
```

```python
import functools
import math

import jax
import jax.numpy as jnp
import numpy as np
from jax import lax
from jax.experimental import pallas as pl
from jax.experimental.pallas import tpu as pltpu
from jax.sharding import Mesh, PartitionSpec as P


@functools.lru_cache(maxsize=None)
def transform_matrices(rows):
    j = np.arange(rows)
    angle = 2 * np.pi * (np.outer(j, j) % rows) / rows
    cos, sin = np.cos(angle), np.sin(angle)
    general = np.block([[cos, sin], [-sin, cos]])
    half = rows // 2
    m = np.arange(half)
    low = 2 * np.pi * (np.outer(m, j) % rows) / rows
    mid = 2 * np.pi * (np.outer(2 * m + 1, j) % (2 * rows)) / (2 * rows)
    zero = np.zeros((half, rows))
    low_sin = -np.sin(low)
    low_sin[0] = np.where(j % 2 == 0, 1.0, -1.0)
    first = np.block(
        [[np.cos(low), zero], [zero, np.cos(mid)], [low_sin, zero], [zero, -np.sin(mid)]]
    )
    both = np.stack([first, general])
    return both.astype(jnp.bfloat16), both.transpose(0, 2, 1).astype(jnp.bfloat16)


@functools.lru_cache(maxsize=None)
def mixing_weights(devices):
    c = np.arange(devices)
    angle = 2 * np.pi * (np.outer(c, c) % (2 * devices)) / (2 * devices)
    real, imag = np.cos(angle), -np.sin(angle)
    imag[0] = np.where(c % 2 == 0, 1.0, -1.0)
    return np.stack([real, imag]).astype(np.float32)


@functools.lru_cache(maxsize=None)
def twists(devices, rows):
    angle = 2 * np.pi * np.outer(np.arange(devices), np.arange(rows)) / (2 * devices * rows)
    return np.stack([np.cos(angle), np.sin(angle)], axis=1).astype(np.float32)


def convolve_kernel(scale, flag, weights, x, forward, inverse, twist, filt, out, total):
    c = pl.program_id(0)
    devices, rows, width = x.shape
    half = rows // 2

    mixed_real = jnp.zeros((rows, width), jnp.float32)
    mixed_imag = jnp.zeros((rows, width), jnp.float32)
    for n in range(devices):
        block = x[n].astype(jnp.float32)
        mixed_real += weights[0, c, n] * block
        mixed_imag += weights[1, c, n] * block
    tc = twist[0, 0]
    ts = twist[0, 1]
    turned = jnp.concatenate(
        [mixed_real * tc + mixed_imag * ts, mixed_imag * tc - mixed_real * ts]
    ).astype(jnp.bfloat16)
    freq = jnp.dot(forward[0], turned, preferred_element_type=jnp.float32)
    swap = flag[0]
    filt_real = jnp.concatenate([filt[0, swap, 0], filt[0, 1 - swap, 0]]).astype(jnp.float32)
    filt_imag = jnp.concatenate([filt[0, swap, 1], filt[0, 1 - swap, 1]]).astype(jnp.float32)
    fr, fi = freq[:rows], freq[rows:]
    single = jnp.logical_and(
        c == 0, lax.broadcasted_iota(jnp.int32, (rows, width), 0) == 0
    )
    cross = fi * filt_imag
    prod_real = fr * filt_real - jnp.where(single, 0.0, cross)
    prod_imag = jnp.where(single, cross, fr * filt_imag + fi * filt_real)
    prod = jnp.concatenate([prod_real, prod_imag]).astype(jnp.bfloat16)
    back = jnp.dot(inverse[0], prod, preferred_element_type=jnp.float32)
    br, bi = back[:rows], back[rows:]
    back_real = (br * tc - bi * ts) * scale
    back_imag = (br * ts + bi * tc) * scale

    @pl.when(c == 0)
    def _():
        for n in range(devices):
            total[n] = weights[0, c, n] * back_real + weights[1, c, n] * back_imag

    @pl.when(c > 0)
    def _():
        for n in range(devices):
            total[n] += weights[0, c, n] * back_real + weights[1, c, n] * back_imag

    @pl.when(c == devices - 1)
    def _():
        out[...] = total[...].astype(out.dtype)


def convolve(x, filt, flag):
    devices, rows, width = x.shape
    forward, inverse = transform_matrices(rows)
    weights = mixing_weights(devices)
    twist = np.broadcast_to(twists(devices, rows)[..., None], (devices, 2, rows, width))
    twist = jnp.asarray(np.ascontiguousarray(twist))
    whole = lambda c: (0, 0, 0)
    matrix = pl.BlockSpec((1, 2 * rows, 2 * rows), lambda c: (jnp.minimum(c, 1), 0, 0))
    return pl.pallas_call(
        functools.partial(convolve_kernel, 1.0 / (2 * devices * rows)),
        grid=(devices,),
        in_specs=[
            pl.BlockSpec(memory_space=pltpu.SMEM),
            pl.BlockSpec(memory_space=pltpu.SMEM),
            pl.BlockSpec((devices, rows, width), whole),
            matrix,
            matrix,
            pl.BlockSpec((1, 2, rows, width), lambda c: (c, 0, 0, 0)),
            pl.BlockSpec((1, 2, 2, rows // 2, width), lambda c: (c, 0, 0, 0, 0)),
        ],
        out_specs=pl.BlockSpec((devices, rows, width), whole),
        out_shape=jax.ShapeDtypeStruct((devices, rows, width), jnp.bfloat16),
        scratch_shapes=[pltpu.VMEM((devices, rows, width), jnp.float32)],
        compiler_params=pltpu.CompilerParams(vmem_limit_bytes=56 * 2**20),
        cost_estimate=pl.CostEstimate(
            flops=16 * devices * rows * rows * width,
            bytes_accessed=16 * 2**20,
            transcendentals=0,
        ),
    )(flag, jnp.asarray(weights), x, jnp.asarray(forward), jnp.asarray(inverse), twist, filt)


def fold_filters(spectrum):
    hi, lo, position = lax.axis_index("hi"), lax.axis_index("lo"), lax.axis_index("ctx")
    devices = lax.axis_size("ctx")
    block = spectrum.shape[1]
    width = spectrum.shape[2] // 2
    first, second = spectrum[:, :, :width], spectrum[:, :, width:]
    upper = hi == 1
    kept = jnp.where(upper, second, first)
    sent = jnp.where(upper, first, second)
    got = lax.ppermute(sent, ("hi", "lo"), [(f, 3 - f) for f in range(4)])
    slot_a = jnp.where(upper, got, kept)
    slot_b = jnp.where(upper, kept, got)
    half = jnp.bitwise_xor(hi, lo)
    passed = jnp.where(half == 0, slot_b, slot_a)
    swapped = lax.ppermute(
        passed, ("ctx", "hi", "lo"), [(0, 1), (1, 0), (2, 3), (3, 2)]
    )
    edge = position == 0
    base = jnp.where(jnp.logical_and(edge, half == 1), slot_b, slot_a)
    mirrored = jnp.where(edge, swapped, slot_b)
    wrap = jnp.logical_and(edge, half == 0)
    row = lax.broadcasted_iota(jnp.int32, (block, block), 0)
    col = lax.broadcasted_iota(jnp.int32, (block, block), 1)
    flip = (row + col == jnp.where(wrap, block, block - 1)).astype(jnp.bfloat16)
    turned = jnp.einsum("ij,rjk->rik", flip, mirrored, preferred_element_type=jnp.float32)
    real = base[0].astype(jnp.float32) + turned[0]
    imag = base[1].astype(jnp.float32) - turned[1]
    at_edge = jnp.logical_and(wrap, lax.broadcasted_iota(jnp.int32, (block, 1), 0) == 0)
    imag = jnp.where(at_edge, mirrored[0, :1].astype(jnp.float32), imag)
    return jnp.stack([real, imag]).astype(jnp.bfloat16)


def fused_kernel(scale, weights, gate_in, values, gate_out, bias, spectrum, forward_in, inverse_in,
                 twist_in, out, sequence, filt, mixed, kept, got, swapped, pair, folded, forward,
                 inverse, twist, freq, total, leaving, arrived, kept_sem, far_send, far_recv,
                 swap_send, swap_recv, fold_send, fold_recv, mix_send, mix_recv, back_send,
                 back_recv, table_sem):
    me, hi, lo = lax.axis_index("ctx"), lax.axis_index("hi"), lax.axis_index("lo")
    devices, rows, width = sequence.shape
    block = spectrum.shape[1]
    group = devices * width
    edge = me == 0
    half = (hi + lo) % 2

    def offset(t):
        step = (t + 1) // 2
        return devices // 2 + (1 - 2 * (t % 2)) * step

    def target(t):
        return (me + offset(t)) % devices

    def origin(t):
        return (me + devices - offset(t)) % devices

    def columns(side, c, l):
        start = side * (2 * group) + l * group + c * width
        return spectrum.at[:, :, pl.ds(pl.multiple_of(start, 128), width)]

    def remote(src, dst, send, recv, target):
        return pltpu.make_async_remote_copy(
            src_ref=src, dst_ref=dst, send_sem=send, recv_sem=recv,
            device_id=target, device_id_type=pl.DeviceIdType.MESH,
        )

    def keep(c, l):
        return pltpu.make_async_copy(columns(hi, c, l), kept.at[c, l], kept_sem.at[c, l])

    def far(c, l):
        return remote(columns(1 - hi, c, l), got.at[c, l], far_send.at[c, l], far_recv.at[c, l],
                      (me, 1 - hi, 1 - lo))

    def swap(source, c, l):
        return remote(source.at[c, l], swapped.at[c, l], swap_send.at[c, l], swap_recv.at[c, l],
                      (me, hi, 1 - lo))

    def fold(c, l):
        return remote(folded.at[c, l], filt.at[me, lo], fold_send.at[c, l], fold_recv.at[me, lo],
                      (c, hi, l))

    def fold_here(c, l):
        return pltpu.make_async_copy(folded.at[c, l], filt.at[me, lo], fold_send.at[c, l])

    def mix(c):
        return remote(mixed.at[c], sequence.at[me], mix_send.at[c], mix_recv.at[me], (c, hi, lo))

    def mix_here():
        return pltpu.make_async_copy(mixed.at[me], sequence.at[me], mix_send.at[me])

    def give_back(n):
        return remote(leaving.at[n], arrived.at[me], back_send.at[n], back_recv.at[me],
                      (n, hi, lo))

    tables = [
        pltpu.make_async_copy(src, dst, table_sem.at[i])
        for i, (src, dst) in enumerate(
            ((forward_in, forward), (inverse_in, inverse), (twist_in, twist))
        )
    ]

    barrier = pltpu.get_barrier_semaphore()

    @pl.loop(0, devices)
    def _(c):
        for l in range(2):
            @pl.when(jnp.logical_or(c != me, lo != l))
            def _():
                pl.semaphore_signal(barrier, inc=1, device_id=(c, hi, l),
                                    device_id_type=pl.DeviceIdType.MESH)

    pl.semaphore_signal(barrier, inc=1, device_id=(me, 1 - hi, 1 - lo),
                        device_id_type=pl.DeviceIdType.MESH)

    @pl.loop(0, devices)
    def _(t):
        c = target(t)
        for l in range(2):
            keep(c, l).start()

    @pl.loop(0, devices)
    def _(c):
        place = pl.ds(pl.multiple_of(c * width, 128), width)
        mixed[c] = (
            gate_in[:, place].astype(jnp.float32) * values[:, place].astype(jnp.float32)
        ).astype(jnp.bfloat16)

    pl.semaphore_wait(barrier, 2 * devices)

    @pl.loop(0, devices)
    def _(t):
        c = target(t)

        @pl.when(c != me)
        def _():
            mix(c).start()

        @pl.when(c == me)
        def _():
            mix_here().start()

        for l in range(2):
            far(c, l).start()

    for table in tables:
        table.start()

    wrap = jnp.logical_and(edge, half == 0)
    row = lax.broadcasted_iota(jnp.int32, (block, block), 0)
    col = lax.broadcasted_iota(jnp.int32, (block, block), 1)
    flip = jnp.where(row + col == jnp.where(wrap, block, block - 1), 1.0, 0.0).astype(jnp.bfloat16)
    at_edge = jnp.logical_and(wrap, lax.broadcasted_iota(jnp.int32, (block, width), 0) == 0)
    base_got = jnp.where(edge, lo, hi) == 1

    def fold_step(t):
        c = target(t)
        for l in range(2):
            keep(c, l).wait()

            @pl.when(jnp.logical_and(edge, lo == 1))
            def _():
                swap(kept, c, l).start()

        for l in range(2):
            far(c, l).wait_recv()

            @pl.when(jnp.logical_and(edge, lo == 0))
            def _():
                swap(got, c, l).start()

        for l in range(2):
            @pl.when(edge)
            def _():
                swap(kept, c, l).wait_recv()
                pair[...] = swapped[c, l]

            @pl.when(jnp.logical_and(me != 0, hi == 0))
            def _():
                pair[...] = got[c, l]

            @pl.when(jnp.logical_and(me != 0, hi == 1))
            def _():
                pair[...] = kept[c, l]

            base = jnp.where(base_got, got[c, l].astype(jnp.float32), kept[c, l].astype(jnp.float32))
            turned_real = jnp.dot(flip, pair[0], preferred_element_type=jnp.float32)
            turned_imag = jnp.dot(flip, pair[1], preferred_element_type=jnp.float32)
            real = base[0] + turned_real
            imag = jnp.where(at_edge, pair[0].astype(jnp.float32), base[1] - turned_imag)
            folded[c, l, 0] = real.astype(jnp.bfloat16)
            folded[c, l, 1] = imag.astype(jnp.bfloat16)
            here = jnp.logical_and(c == me, lo == l)

            @pl.when(here)
            def _():
                fold_here(c, l).start()

            @pl.when(jnp.logical_not(here))
            def _():
                fold(c, l).start()

    def forward_step(c):
        real = jnp.zeros((rows, width), jnp.float32)
        imag = jnp.zeros((rows, width), jnp.float32)
        for n in range(devices):
            part = sequence[n].astype(jnp.float32)
            real += weights[0, c, n] * part
            imag += weights[1, c, n] * part
        tc, ts = twist[c, 0], twist[c, 1]
        turned = jnp.concatenate([real * tc + imag * ts, imag * tc - real * ts])
        freq[c] = jnp.dot(
            forward[jnp.minimum(c, 1)], turned.astype(jnp.bfloat16),
            preferred_element_type=jnp.float32,
        )

    def inverse_step(c):
        filt_real = jnp.concatenate([filt[c, hi, 0], filt[c, 1 - hi, 0]]).astype(jnp.float32)
        filt_imag = jnp.concatenate([filt[c, hi, 1], filt[c, 1 - hi, 1]]).astype(jnp.float32)
        fr, fi = freq[c, :rows], freq[c, rows:]
        top = lax.broadcasted_iota(jnp.int32, (rows, width), 0) == 0
        single = jnp.logical_and(c == 0, top)
        cross = fi * filt_imag
        prod_real = fr * filt_real - jnp.where(single, 0.0, cross)
        prod_imag = jnp.where(single, cross, fr * filt_imag + fi * filt_real)
        prod = jnp.concatenate([prod_real, prod_imag]).astype(jnp.bfloat16)
        back = jnp.dot(inverse[jnp.minimum(c, 1)], prod, preferred_element_type=jnp.float32)
        tc, ts = twist[c, 0] * scale, twist[c, 1] * scale
        br, bi = back[:rows], back[rows:]
        real = br * tc - bi * ts
        imag = br * ts + bi * tc
        for n in range(devices):
            total[n] += weights[0, c, n] * real + weights[1, c, n] * imag

    early = devices // 2

    @pl.loop(0, early)
    def _(t):
        fold_step(t)

    for table in tables:
        table.wait()

    @pl.loop(0, devices)
    def _(c):
        total[c] = jnp.zeros((rows, width), jnp.float32)

        @pl.when(c == me)
        def _():
            mix_here().wait()

        @pl.when(c != me)
        def _():
            remote(mixed.at[c], sequence.at[c], mix_send.at[c], mix_recv.at[c],
                   (c, hi, lo)).wait_recv()

    @pl.loop(early, devices)
    def _(t):
        fold_step(t)

        @pl.loop(0, 2)
        def _(i):
            forward_step(2 * (t - early) + i)

    @pl.loop(0, devices)
    def _(s):
        c = origin(s)
        for l in range(2):
            here = jnp.logical_and(c == me, lo == l)

            @pl.when(here)
            def _():
                fold_here(c, l).wait()

            @pl.when(jnp.logical_not(here))
            def _():
                remote(folded.at[c, l], filt.at[c, l], fold_send.at[c, l], fold_recv.at[c, l],
                       (c, hi, l)).wait_recv()

        inverse_step(c)

    @pl.loop(0, devices)
    def _(t):
        n = target(t)
        leaving[n] = total[n].astype(jnp.bfloat16)

        @pl.when(n != me)
        def _():
            give_back(n).start()

    @pl.loop(0, devices)
    def _(s):
        c = origin(s)
        place = pl.ds(pl.multiple_of(c * width, 128), width)

        @pl.when(c == me)
        def _():
            arrived[c] = leaving[c]

        @pl.when(c != me)
        def _():
            remote(leaving.at[c], arrived.at[c], back_send.at[c], back_recv.at[c],
                   (c, hi, lo)).wait_recv()

        skip = bias[:, place] * mixed[c].astype(jnp.float32)
        out[:, place] = (
            gate_out[:, place].astype(jnp.float32) * (arrived[c].astype(jnp.float32) + skip)
        ).astype(out.dtype)

    @pl.loop(0, devices)
    def _(c):
        @pl.when(c != me)
        def _():
            mix(c).wait_send()
            give_back(c).wait_send()

        for l in range(2):
            far(c, l).wait_send()

            @pl.when(edge)
            def _():
                swap(kept, c, l).wait_send()

            @pl.when(jnp.logical_or(c != me, lo != l))
            def _():
                fold(c, l).wait_send()


def fused(gate_in, values, gate_out, bias, spectrum):
    devices = lax.axis_size("ctx")
    rows, channels = gate_in.shape
    width = channels // devices
    block = spectrum.shape[1]
    forward, inverse = transform_matrices(rows)
    twist = np.broadcast_to(twists(devices, rows)[..., None], (devices, 2, rows, width))
    tile = (devices, 2, 2, block, width)
    whole = (devices, rows, width)
    dma = pltpu.SemaphoreType.DMA
    here = pl.BlockSpec(memory_space=pltpu.VMEM)
    anywhere = pl.BlockSpec(memory_space=pl.ANY)
    return pl.pallas_call(
        functools.partial(fused_kernel, 1.0 / (2 * devices * rows)),
        in_specs=[pl.BlockSpec(memory_space=pltpu.SMEM)] + [here] * 4 + [anywhere] * 4,
        out_specs=here,
        out_shape=jax.ShapeDtypeStruct((rows, channels), jnp.bfloat16),
        scratch_shapes=[
            pltpu.VMEM(whole, jnp.bfloat16),
            pltpu.VMEM(tile, jnp.bfloat16),
            pltpu.VMEM(whole, jnp.bfloat16),
            pltpu.VMEM(tile, jnp.bfloat16),
            pltpu.VMEM(tile, jnp.bfloat16),
            pltpu.VMEM(tile, jnp.bfloat16),
            pltpu.VMEM((2, block, width), jnp.bfloat16),
            pltpu.VMEM(tile, jnp.bfloat16),
            pltpu.VMEM((2, 2 * rows, 2 * rows), jnp.bfloat16),
            pltpu.VMEM((2, 2 * rows, 2 * rows), jnp.bfloat16),
            pltpu.VMEM((devices, 2, rows, width), jnp.float32),
            pltpu.VMEM((devices, 2 * rows, width), jnp.float32),
            pltpu.VMEM(whole, jnp.float32),
            pltpu.VMEM(whole, jnp.bfloat16),
            pltpu.VMEM(whole, jnp.bfloat16),
            *[dma((devices, 2))] * 7,
            *[dma((devices,))] * 4,
            dma((3,)),
        ],
        compiler_params=pltpu.CompilerParams(
            collective_id=0, has_side_effects=True, vmem_limit_bytes=58 * 2**20
        ),
        cost_estimate=pl.CostEstimate(
            flops=16 * devices * rows * rows * width + 10**9,
            bytes_accessed=24 * 2**20,
            transcendentals=0,
        ),
    )(
        jnp.asarray(mixing_weights(devices)), gate_in, values, gate_out, bias.reshape(1, channels),
        spectrum, jnp.asarray(forward), jnp.asarray(inverse),
        jnp.asarray(np.ascontiguousarray(twist)),
    )


def exchange_small(mixed, spectrum):
    devices = lax.axis_size("ctx")
    rows, channels = mixed.shape
    width = channels // devices
    parts = mixed.reshape(rows, devices, width).transpose(1, 0, 2)
    sequence = lax.all_to_all(parts, "ctx", split_axis=0, concat_axis=0, tiled=True)

    folded = fold_filters(spectrum)
    block = folded.shape[1]
    pieces = folded.reshape(2, block, 2, devices, width).transpose(3, 2, 0, 1, 4)
    pieces = pieces.reshape(devices * 2, 2, block, width)
    filt = lax.all_to_all(pieces, ("ctx", "lo"), split_axis=0, concat_axis=0, tiled=True)
    filt = filt.reshape(devices, 2, 2, block, width)
    return sequence, filt


def body(gate_in, values, gate_out, bias, spectrum):
    devices = lax.axis_size("ctx")
    rows, channels = gate_in.shape
    width = channels // devices
    if width % 128 == 0:
        return fused(gate_in, values, gate_out, bias, spectrum)
    mixed = (gate_in.astype(jnp.float32) * values.astype(jnp.float32)).astype(jnp.bfloat16)
    mixed = lax.optimization_barrier(mixed)
    sequence, filt = exchange_small(mixed, spectrum)
    flag = lax.axis_index("hi").astype(jnp.int32).reshape(1)

    convolved = convolve(sequence, filt, flag)
    back = lax.all_to_all(convolved, "ctx", split_axis=0, concat_axis=0, tiled=True)
    back = back.transpose(1, 0, 2).reshape(rows, channels).astype(jnp.float32)
    total = back + bias[None, :] * mixed.astype(jnp.float32)
    return (gate_out.astype(jnp.float32) * total).astype(jnp.bfloat16)


def solution(mesh):
    ctx, fsdp = mesh.devices.shape
    split = Mesh(mesh.devices.reshape(ctx, fsdp // 2, 2), ("ctx", "hi", "lo"))
    tokens = P("ctx", ("hi", "lo"))
    return jax.shard_map(
        body,
        mesh=split,
        in_specs=(
            tokens,
            tokens,
            tokens,
            P(("hi", "lo")),
            P(None, ("ctx", "hi", "lo"), None),
        ),
        out_specs=tokens,
        check_vma=False,
    )
```
